128 devices in a mesh: group: 2 (over y_lo), resp: 8 (over y_hi, z), tensor: 8 (over x, core).
Axes of the slice: x: 4, y: 4 (y_hi: 2, y_lo: 2; y = y_hi * 2 + y_lo), z: 4, core: 2. Of those that a mesh axis runs over, the one named last changes fastest.
Arguments:
- queries: bfloat16 [16, 512, 8192], P(('group', 'resp'), None, 'tensor'), parts along dimension 0, may hold values from -50 to 50
- resp_keys: bfloat16 [16, 512, 1024], P(('group', 'resp'), None, 'tensor'), parts along dimension 0, may hold values from -6 to 6
- resp_values: bfloat16 [16, 512, 1024], P(('group', 'resp'), None, 'tensor'), parts along dimension 0, may hold values from -6 to 6
- prompt_keys: bfloat16 [4096, 1024], P(('group', 'resp', 'tensor')), parts along dimension 0, may hold values from -7 to 7
- prompt_values: bfloat16 [4096, 1024], P(('group', 'resp', 'tensor')), parts along dimension 0, may hold values from -6 to 6
- out_grad: bfloat16 [16, 512, 8192], P(('group', 'resp'), None, 'tensor'), parts along dimension 0, may hold values from -6 to 6
- lengths: int32 [16], P(('group', 'resp')), parts along dimension 0, may hold values from 1 to 512, 2560 in all
Outputs:
- attended: bfloat16 [16, 512, 8192], P(('group', 'resp'), None, 'tensor'), parts along dimension 0
- query_grad: bfloat16 [16, 512, 8192], P(('group', 'resp'), None, 'tensor'), parts along dimension 0
- resp_key_grad: bfloat16 [16, 512, 1024], P(('group', 'resp'), None, 'tensor'), parts along dimension 0
- resp_value_grad: bfloat16 [16, 512, 1024], P(('group', 'resp'), None, 'tensor'), parts along dimension 0
- prompt_key_grad: float32 [4096, 1024], P(('group', 'resp', 'tensor')), parts along dimension 0
- prompt_value_grad: float32 [4096, 1024], P(('group', 'resp', 'tensor')), parts along dimension 0
The draws below stay inside these ranges and needn't reach their ends.
There are 2 independent parts, one for each index of `group`. The reference program is written for one: setup_inputs(seed, part) draws one part's arguments, and reference() takes and returns one part's arrays. A program takes and returns all parts, laid end to end along the dimension named above; each array names one. Nothing has to cross between parts.
Inputs may be any that keep to these rules, and one draw needn't show every extreme that they name: For each prompt group separately, its 8 lengths sum to 2560, and one of them is exactly 512; the table lists the groups one after another.
All inputs are finite; a program needn't handle non-finite values.
Results may differ from the reference program's by a relative error of at most 0.012.
The reference program's roundings to bfloat16 on the way count: a program that leaves them out, or rounds other values in their place, can miss the bound.
Values may be sent and summed in bfloat16 or wider, within the bound.
A program may use at most 64 MiB of HBM per device.

```python
import math
import jax
import jax.numpy as jnp
import numpy as np
from jax import lax

QH = 64
KVH = 8
HD = 128
PROMPT = 2048
RLEN = 512
RESPONSES = 8


def shared_keys(key, pair_share):
    key_normal = jax.random.fold_in(key, 0)
    gaussian = jnp.clip(jax.random.normal(key_normal, (PROMPT, KVH * HD), jnp.float32), -6.0, 6.0)
    raw_keys = gaussian
    row_ids = jnp.arange(PROMPT)
    follower = (row_ids % 16 == 1).astype(jnp.float32)[:, None] * pair_share
    return (1.0 - follower) * raw_keys


def draw_prompt_keys(key, part):
    base_keys = shared_keys(key, 0.0)
    return base_keys.astype(jnp.bfloat16)


def draw_queries(key, part):
    key = jax.random.fold_in(key, 23)
    key_drawn = jax.random.fold_in(key, 0)
    result = jnp.clip(2.0 * jax.random.normal(key_drawn, (RESPONSES, RLEN, QH, HD), jnp.float32), -12.0, 12.0)
    return result.reshape(RESPONSES, RLEN, QH * HD).astype(jnp.bfloat16)


def level_of(key, shape, shards, smallest, top_value):
    level = 1.0
    for axis_at, blocks in shards:
        draws = jax.random.uniform(jax.random.fold_in(jax.random.fold_in(key, 6), axis_at), (blocks,), jnp.float32, smallest / len(shards), top_value / len(shards))
        level = level * jnp.repeat(jnp.exp(draws), shape[axis_at] // blocks).reshape((-1,) + (1,) * (len(shape) - 1 - axis_at))
    return level


def profile(number_of, total, bound, skew):
    loads = [(1 << 20) // math.isqrt(rank ** skew) + 1 for rank in range(2, number_of + 1)]
    surplus, counts = total - bound - (number_of - 1), [1] * (number_of - 1)
    while surplus > 0:
        movable = [i for i in range(number_of - 1) if counts[i] < bound]
        pool, budget = sum([loads[i] for i in movable]), surplus
        for i in movable:
            extra = min(bound - counts[i], max(1, budget * loads[i] // pool), surplus)
            counts[i] = counts[i] + extra
            surplus = surplus - extra
    return np.array([bound] + counts)


def uneven_parts(stream_key, count, total, limit, slope):
    if count == 2:
        one = jax.random.randint(stream_key, (), max(1, total - limit), min(limit, total - 1) + 1)
        return jnp.stack([one, total - one])
    sizes = jnp.asarray(profile(count, total, limit, slope), jnp.int32)
    couples = (count - 1) // 2
    giver, taker = sizes[1:1 + 2 * couples:2], sizes[2:2 + 2 * couples:2]
    margin = jnp.minimum(giver - 1, limit - taker)
    moved = jax.random.randint(jax.random.fold_in(stream_key, 1), (couples,), 0, 1 << 20) % (margin + 1)
    sizes = sizes.at[1:1 + 2 * couples:2].set(giver - moved).at[2:2 + 2 * couples:2].set(taker + moved)
    return sizes[jax.random.permutation(jax.random.fold_in(stream_key, 2), count)]


def noise(stream_key, extent, spread, reach, cuts=(), kind=jnp.bfloat16):
    values = spread * jax.random.normal(stream_key, extent, jnp.float32)
    if cuts:
        values = values * level_of(stream_key, extent, cuts, -0.22, 0.18)
    return jnp.clip(values, -reach, reach).astype(kind)


def setup_inputs(seed: int = 0, part: int = 0) -> dict:
    keys = jax.random.split(jax.random.key(seed), 8)
    part_splits = jax.random.split(jax.random.fold_in(keys[7], part), 8)
    queries = draw_queries(jax.random.fold_in(jax.random.fold_in(keys[7], part), 71), part)
    resp_keys = noise(part_splits[1], (RESPONSES, RLEN, KVH * HD), 1.0, 6.0, ((0, 8), (2, 8)))
    resp_values = noise(part_splits[2], (RESPONSES, RLEN, KVH * HD), 1.0, 6.0, ((0, 8), (2, 8)))
    prompt_keys = draw_prompt_keys(jax.random.fold_in(jax.random.fold_in(keys[7], part), 71), part)
    prompt_values = noise(part_splits[4], (PROMPT, KVH * HD), 1.0, 6.0, ((0, 64),))
    out_grad = noise(part_splits[5], (RESPONSES, RLEN, QH * HD), 1.0, 6.0, ((0, 8), (2, 8)))
    lengths = uneven_parts(part_splits[6], RESPONSES, RESPONSES * 5 * RLEN // 8, RLEN, 1).astype(jnp.int32)
    return dict(queries=queries, resp_keys=resp_keys, resp_values=resp_values, prompt_keys=prompt_keys, prompt_values=prompt_values, out_grad=out_grad, lengths=lengths)


def rounded(values):
    return lax.optimization_barrier(values.astype(jnp.bfloat16)).astype(jnp.float32)


def pair_terms(query_rows, grad_rows, key_resp, value_resp, key_prompt, value_prompt, resp_length):
    factor = HD ** -0.5
    positions = jnp.arange(RLEN, dtype=jnp.int32)
    live_rows = positions < resp_length
    allowed = (positions[None, :] <= positions[:, None]) & (positions[None, :] < resp_length)
    query_wide = query_rows.astype(jnp.float32)
    key_prompt_wide = key_prompt.astype(jnp.float32)
    value_prompt_wide = value_prompt.astype(jnp.float32)
    key_resp_wide = key_resp.astype(jnp.float32)
    value_resp_wide = value_resp.astype(jnp.float32)
    score_prompt = jnp.einsum("gqd,kd->gqk", query_wide, key_prompt_wide) * factor
    score_resp = jnp.where(allowed[None], jnp.einsum("gqd,kd->gqk", query_wide, key_resp_wide) * factor, -jnp.inf)
    row_top = jnp.maximum(jnp.max(score_prompt, -1), jnp.max(score_resp, -1))
    exp_prompt = jnp.exp(score_prompt - row_top[..., None])
    exp_resp = jnp.exp(score_resp - row_top[..., None])
    row_total = jnp.sum(exp_prompt, -1) + jnp.sum(exp_resp, -1)
    frac_prompt = exp_prompt / row_total[..., None]
    frac_resp = exp_resp / row_total[..., None]
    weight_prompt = rounded(frac_prompt)
    weight_resp = rounded(frac_resp)
    mixture = jnp.einsum("gqk,kd->gqd", weight_prompt, value_prompt_wide) + jnp.einsum("gqk,kd->gqd", weight_resp, value_resp_wide)
    attended = jnp.where(live_rows[None, :, None], mixture, 0.0).astype(jnp.bfloat16)
    live_grad = jnp.where(live_rows[None, :, None], grad_rows, jnp.zeros_like(grad_rows)).astype(jnp.float32)
    row_delta = jnp.sum(live_grad * lax.optimization_barrier(attended).astype(jnp.float32), -1)
    sgrad_prompt = rounded(frac_prompt * (jnp.einsum("gqd,kd->gqk", live_grad, value_prompt_wide) - row_delta[..., None]))
    sgrad_resp = rounded(frac_resp * (jnp.einsum("gqd,kd->gqk", live_grad, value_resp_wide) - row_delta[..., None]))
    query_grad = (factor * (jnp.einsum("gqk,kd->gqd", sgrad_prompt, key_prompt_wide) + jnp.einsum("gqk,kd->gqd", sgrad_resp, key_resp_wide))).astype(jnp.bfloat16)
    key_grad_resp = factor * jnp.einsum("gqk,gqd->kd", sgrad_resp, query_wide)
    value_grad_resp = jnp.einsum("gqk,gqd->kd", weight_resp, live_grad)
    key_grad_prompt = factor * jnp.einsum("gqk,gqd->kd", sgrad_prompt, query_wide)
    value_grad_prompt = jnp.einsum("gqk,gqd->kd", weight_prompt, live_grad)
    return attended, query_grad, key_grad_resp, value_grad_resp, key_grad_prompt, value_grad_prompt


def reference(queries, resp_keys, resp_values, prompt_keys, prompt_values, out_grad, lengths):
    heads_per = QH // KVH
    query_blocks = queries.reshape(RESPONSES, RLEN, KVH, heads_per, HD).transpose(0, 2, 3, 1, 4)
    grad_blocks = out_grad.reshape(RESPONSES, RLEN, KVH, heads_per, HD).transpose(0, 2, 3, 1, 4)
    key_blocks = resp_keys.reshape(RESPONSES, RLEN, KVH, HD).transpose(0, 2, 1, 3)
    value_blocks = resp_values.reshape(RESPONSES, RLEN, KVH, HD).transpose(0, 2, 1, 3)
    prompt_key_heads = prompt_keys.reshape(PROMPT, KVH, HD).transpose(1, 0, 2)
    prompt_value_heads = prompt_values.reshape(PROMPT, KVH, HD).transpose(1, 0, 2)

    def per_response(sums, inputs):
        query_set, grad_set, key_set, value_set, resp_length = inputs

        def per_head(pieces):
            return pair_terms(pieces[0], pieces[1], pieces[2], pieces[3], pieces[4], pieces[5], resp_length)

        results = lax.map(per_head, (query_set, grad_set, key_set, value_set, prompt_key_heads, prompt_value_heads))
        new_sums = (sums[0] + results[4], sums[1] + results[5])
        return new_sums, (results[0], results[1], results[2], results[3])

    start_sums = (jnp.zeros((KVH, PROMPT, HD), jnp.float32), jnp.zeros((KVH, PROMPT, HD), jnp.float32))
    final_sums, outputs = lax.scan(per_response, start_sums, (query_blocks, grad_blocks, key_blocks, value_blocks, lengths))
    attended = outputs[0].transpose(0, 3, 1, 2, 4).reshape(RESPONSES, RLEN, QH * HD)
    query_grad = outputs[1].transpose(0, 3, 1, 2, 4).reshape(RESPONSES, RLEN, QH * HD)
    resp_key_grad = outputs[2].transpose(0, 2, 1, 3).reshape(RESPONSES, RLEN, KVH * HD).astype(jnp.bfloat16)
    resp_value_grad = outputs[3].transpose(0, 2, 1, 3).reshape(RESPONSES, RLEN, KVH * HD).astype(jnp.bfloat16)
    prompt_key_grad = final_sums[0].transpose(1, 0, 2).reshape(PROMPT, KVH * HD)
    prompt_value_grad = final_sums[1].transpose(1, 0, 2).reshape(PROMPT, KVH * HD)
    return attended, query_grad, resp_key_grad, resp_value_grad, prompt_key_grad, prompt_value_grad
```

```python
import functools
import math

import jax
import jax.numpy as jnp
from jax import lax
from jax.experimental import pallas as pl
from jax.experimental.pallas import tpu as pltpu
from jax.sharding import PartitionSpec as P

HD = 128
CHUNK = 256
PAIR = 2
ONES = 16
SCALE = HD**-0.5
LOG_SCALE = SCALE / math.log(2.0)
BF16 = jnp.bfloat16
F32 = jnp.float32
MESH = pl.DeviceIdType.MESH


def mm(left, right):
    return jnp.dot(left, right, preferred_element_type=F32)


def by_tile(op, wide, stat):
    rows, lanes = wide.shape
    return op(wide.reshape(rows // 8, 8, lanes), stat[None]).reshape(rows, lanes)


def top_of(wide):
    rows, lanes = wide.shape
    return jnp.max(wide.reshape(rows // 8, 8, lanes), axis=0)


def hop(step, z_size):
    inner = step % z_size
    return step // z_size, ((inner + 1) // 2) * (2 * (inner % 2) - 1)


def kernel(
    sizes,
    length_ref,
    q_hbm,
    g_hbm,
    rk_hbm,
    rv_hbm,
    pk_hbm,
    pv_hbm,
    att_hbm,
    dq_hbm,
    drk_ref,
    drv_ref,
    dpk_ref,
    dpv_ref,
    q,
    g,
    rk,
    rv,
    q_t,
    g_t,
    k_t,
    v_t,
    k_two,
    cache,
    weights,
    tops,
    top,
    inv_total,
    delta,
    out_t,
    dq_t,
    att,
    dq,
    score_buf,
    w_buf,
    ds_buf,
    stat_a,
    stat_b,
    acc,
    send_buf,
    recv_buf,
    total,
    in_sem,
    out_sem,
    a_send,
    a_recv,
    b_send,
    b_recv,
    c_send,
    c_recv,
    d_send,
    d_recv,
):
    n_resp, n_tensor, z_size, heads = sizes
    y_size = n_resp // z_size
    seq = q.shape[0]
    share = pk_hbm.shape[0]
    resp = lax.axis_index("resp")
    tensor = lax.axis_index("tensor")
    y, z = resp // z_size, resp % z_size

    def sends_to(step):
        dy, dz = hop(step, z_size)
        return ((y + dy) % y_size) * z_size + (z + dz + z_size) % z_size

    def comes_from(step):
        dy, dz = hop(step, z_size)
        return ((y - dy + y_size) % y_size) * z_size + (z - dz + z_size) % z_size

    def columns(index):
        return pl.ds(pl.multiple_of(index * HD, HD), HD)

    def part(index):
        return pl.ds(pl.multiple_of(index * share, share), share)

    loads = [
        pltpu.make_async_copy(source, target, in_sem.at[index])
        for index, (source, target) in enumerate(
            (
                (q_hbm, q),
                (g_hbm, g),
                (rk_hbm, rk),
                (rv_hbm, rv),
                (pk_hbm.at[:, columns(tensor)], cache.at[resp, 0, part(tensor)]),
                (pv_hbm.at[:, columns(tensor)], cache.at[resp, 1, part(tensor)]),
            )
        )
    ]
    for load in loads:
        load.start()

    barrier = pltpu.get_barrier_semaphore()

    def greet_tensor(step, carry):
        pl.semaphore_signal(
            barrier, inc=1, device_id={"tensor": (tensor + step) % n_tensor}, device_id_type=MESH
        )
        return carry

    def greet_resp(step, carry):
        pl.semaphore_signal(
            barrier, inc=1, device_id={"resp": sends_to(step)}, device_id_type=MESH
        )
        return carry

    lax.fori_loop(1, n_tensor, greet_tensor, 0)
    lax.fori_loop(1, n_resp, greet_resp, 0)
    pl.semaphore_wait(barrier, n_tensor - 1 + n_resp - 1)

    def spread(step, which):
        peer = (tensor + step) % n_tensor
        source = (pk_hbm, pv_hbm)[which]
        return pltpu.make_async_remote_copy(
            src_ref=source.at[:, columns(peer)],
            dst_ref=cache.at[resp, which, part(tensor)],
            send_sem=a_send.at[step, which],
            recv_sem=a_recv.at[step, which],
            device_id={"tensor": peer},
            device_id_type=MESH,
        )

    def gather(step):
        return pltpu.make_async_remote_copy(
            src_ref=cache.at[resp],
            dst_ref=cache.at[resp],
            send_sem=b_send.at[step],
            recv_sem=b_recv.at[step],
            device_id={"resp": sends_to(step)},
            device_id_type=MESH,
        )

    def start_spread(step, carry):
        spread(step, 0).start()
        spread(step, 1).start()
        return carry

    lax.fori_loop(1, n_tensor, start_spread, 0)

    length = length_ref[0]
    live_rows = lax.broadcasted_iota(jnp.int32, (seq, 1), 0) < length
    live_lanes = lax.broadcasted_iota(jnp.int32, (1, seq), 1) < length

    for load in loads:
        load.wait()

    def prepare_head(head, carry):
        wide = q[:, columns(head)].astype(F32).T * LOG_SCALE
        high = wide.astype(BF16)
        q_t[head, 0:HD] = high
        q_t[head, HD:] = (wide - high.astype(F32)).astype(BF16)
        live = jnp.where(live_rows, g[:, columns(head)], jnp.zeros((), BF16))
        g[:, columns(head)] = live
        g_t[head] = live.T
        return carry

    lax.fori_loop(0, heads, prepare_head, 0)

    def wait_spread(step, carry):
        spread(step, 0).wait()
        spread(step, 1).wait()
        return carry

    lax.fori_loop(1, n_tensor, wait_spread, 0)

    def start_gather(step, carry):
        gather(step).start()
        return carry

    lax.fori_loop(1, n_resp, start_gather, 0)

    def prepare_keys(step, keys, values):
        k_t[step] = keys.T
        v_t[step, 0:HD] = values.T
        v_t[step, HD:] = jnp.ones((ONES, CHUNK), BF16)
        rows = pl.ds(pl.multiple_of(step * CHUNK, CHUNK), CHUNK)
        k_two[rows, 0:HD] = keys
        k_two[rows, HD:] = keys

    key_at = lax.broadcasted_iota(jnp.int32, (CHUNK, CHUNK), 0)
    row_at = lax.broadcasted_iota(jnp.int32, (CHUNK, CHUNK), 1)
    seen = key_at <= row_at

    blocks = seq // CHUNK
    for block in range(blocks):
        rows = slice(block * CHUNK, (block + 1) * CHUNK)
        prepare_keys(n_resp + block, rk[rows, :], rv[rows, :])

    def staged(stages):
        depth = len(stages)
        for turn in range(heads + depth - 1):
            for late, stage in enumerate(stages):
                if 0 <= turn - late < heads:
                    stage(turn - late)

    def own_scores(head):
        slot = head % 2
        tops_of = [None] * blocks
        for block in range(blocks):
            for lane in range(block, blocks):
                lanes = slice(lane * CHUNK, (lane + 1) * CHUNK)
                rows = slice(block * CHUNK, (block + 1) * CHUNK)
                at = (n_resp + block) * CHUNK
                score = mm(k_two[at : at + CHUNK, :], q_t[head, :, lanes])
                if lane == block:
                    score = jnp.where(seen, score, -jnp.inf)
                score_buf[slot, rows, lanes] = score
                block_top = top_of(score)
                old = tops_of[lane]
                tops_of[lane] = block_top if old is None else jnp.maximum(old, block_top)
        highest = jnp.concatenate(tops_of, axis=1)
        highest = jnp.broadcast_to(jnp.max(highest, axis=0, keepdims=True), highest.shape)
        top[head] = highest
        for block in range(blocks):
            tops[n_resp + block, head] = highest

    def own_weights(head):
        slot = head % 2
        for block in range(blocks):
            lanes = slice(block * CHUNK, seq)
            rows = slice(block * CHUNK, (block + 1) * CHUNK)
            shift = tops[n_resp + block, head, :, lanes]
            power = jnp.exp2(by_tile(jnp.subtract, score_buf[slot, rows, lanes], shift))
            weights[n_resp + block, head, :, lanes] = power.astype(BF16)

    def own_mix(head):
        for block in range(blocks):
            lanes = slice(block * CHUNK, seq)
            term = mm(v_t[n_resp + block], weights[n_resp + block, head, :, lanes])
            if block == 0:
                out_t[head] = term
            else:
                out_t[head, :, lanes] += term

    staged((own_scores, own_weights, own_mix))

    def forward(turn, carry):
        first = turn * PAIR
        for index in range(PAIR):
            step = first + index

            @pl.when(step > 0)
            def _():
                gather(step).wait_recv()

            source = comes_from(step)
            prepare_keys(step, cache[source, 0], cache[source, 1])

        def scores(head):
            slot = head % 2
            highest = None
            for index in range(PAIR):
                at = pl.ds(pl.multiple_of((first + index) * CHUNK, CHUNK), CHUNK)
                score = mm(k_two[at, :], q_t[head])
                score_buf[slot, index * CHUNK : (index + 1) * CHUNK] = score
                block_top = top_of(score)
                highest = block_top if highest is None else jnp.maximum(highest, block_top)
            old = top[head]
            new = jnp.maximum(old, jnp.max(highest, axis=0, keepdims=True))
            top[head] = new
            stat_a[slot] = jnp.exp2(old - new)
            for index in range(PAIR):
                tops[first + index, head] = new

        def powers(head):
            slot = head % 2
            shift = tops[first, head]
            for index in range(PAIR):
                score = score_buf[slot, index * CHUNK : (index + 1) * CHUNK]
                power = jnp.exp2(by_tile(jnp.subtract, score, shift))
                weights[first + index, head] = power.astype(BF16)
            stat_b[slot] = stat_a[slot]

        def mix(head):
            term = mm(v_t[first], weights[first, head])
            for index in range(1, PAIR):
                term = term + mm(v_t[first + index], weights[first + index, head])
            out_t[head] = by_tile(jnp.multiply, out_t[head], stat_b[head % 2]) + term

        staged((scores, powers, mix))
        return carry

    lax.fori_loop(0, n_resp // PAIR, forward, 0)

    def close_head(head, carry):
        inverse = 1.0 / out_t[head, HD : HD + 1]
        inv_total[head] = jnp.broadcast_to(inverse, (8, seq))
        done = jnp.where(live_lanes, out_t[head, 0:HD] * inverse, 0.0).astype(BF16)
        row_delta = jnp.sum(
            done.astype(F32) * g_t[head].astype(F32), axis=0, keepdims=True
        )
        delta[head] = jnp.broadcast_to(row_delta, (8, seq))
        att[:, columns(head)] = done.T
        dq_t[head] = jnp.zeros((HD, seq), F32)
        return carry

    lax.fori_loop(0, heads, close_head, 0)
    att_out = pltpu.make_async_copy(att, att_hbm, out_sem.at[0])
    att_out.start()

    def backward_chunk(step, values, low):
        lanes = slice(low, seq)
        width = seq - low

        def products(head):
            slot = head % 2
            score_buf[slot, 0:CHUNK, 0:width] = mm(values, g_t[head, :, lanes])
            stat_a[slot, :, 0:width] = (
                jnp.exp2(tops[step, head, :, lanes] - top[head, :, lanes])
                * inv_total[head, :, lanes]
            )

        def grads(head):
            slot = head % 2
            weight = by_tile(
                jnp.multiply,
                weights[step, head, :, lanes].astype(F32),
                stat_a[slot, :, 0:width],
            )
            w_buf[slot, :, 0:width] = weight.astype(BF16)
            gap = by_tile(
                jnp.subtract, score_buf[slot, 0:CHUNK, 0:width], delta[head, :, lanes]
            )
            ds_buf[slot, :, 0:width] = (weight * gap).astype(BF16)

        def terms(head):
            slot = head % 2
            score_grad = ds_buf[slot, :, 0:width]
            dq_t[head, :, lanes] += mm(k_t[step], score_grad)
            at = slice(head * HD, (head + 1) * HD)
            key_term = mm(score_grad, q[lanes, at])
            value_term = mm(w_buf[slot, :, 0:width], g[lanes, at])
            if head == 0:
                acc[0] = key_term
                acc[1] = value_term
            else:
                acc[0] += key_term
                acc[1] += value_term

        staged((products, grads, terms))

    def collect(step):
        return pltpu.make_async_remote_copy(
            src_ref=send_buf.at[step],
            dst_ref=recv_buf.at[step],
            send_sem=c_send.at[step],
            recv_sem=c_recv.at[step],
            device_id={"resp": comes_from(step)},
            device_id_type=MESH,
        )

    def backward(turn, carry):
        step = n_resp - 1 - turn
        backward_chunk(step, cache[comes_from(step), 1], 0)

        @pl.when(step > 0)
        def _():
            send_buf[step, 0] = (acc[0] * SCALE).astype(BF16)
            send_buf[step, 1] = acc[1].astype(BF16)
            collect(step).start()

        @pl.when(step == 0)
        def _():
            total[0] = acc[0] * SCALE
            total[1] = acc[1]

        return carry

    lax.fori_loop(0, n_resp, backward, 0)

    for block in range(blocks):
        rows = slice(block * CHUNK, (block + 1) * CHUNK)
        backward_chunk(n_resp + block, rv[rows, :], block * CHUNK)
        drk_ref[rows, :] = (acc[0] * SCALE).astype(BF16)
        drv_ref[rows, :] = acc[1].astype(BF16)

    def add_part(step, carry):
        collect(step).wait()
        total[0] += recv_buf[step, 0].astype(F32)
        total[1] += recv_buf[step, 1].astype(F32)
        return carry

    lax.fori_loop(1, n_resp, add_part, 0)

    def give_back(step, which):
        peer = (tensor + step) % n_tensor
        target = (dpk_ref, dpv_ref)[which]
        return pltpu.make_async_remote_copy(
            src_ref=total.at[which, part(peer)],
            dst_ref=target.at[:, columns(tensor)],
            send_sem=d_send.at[step, which],
            recv_sem=d_recv.at[step, which],
            device_id={"tensor": peer},
            device_id_type=MESH,
        )

    def start_give(step, carry):
        give_back(step, 0).start()
        give_back(step, 1).start()
        return carry

    lax.fori_loop(1, n_tensor, start_give, 0)
    dpk_ref[:, columns(tensor)] = total[0, part(tensor), :]
    dpv_ref[:, columns(tensor)] = total[1, part(tensor), :]

    def close_query(head, carry):
        dq[:, columns(head)] = (dq_t[head] * SCALE).astype(BF16).T
        return carry

    lax.fori_loop(0, heads, close_query, 0)
    dq_out = pltpu.make_async_copy(dq, dq_hbm, out_sem.at[1])
    dq_out.start()

    def wait_give(step, carry):
        give_back(step, 0).wait()
        give_back(step, 1).wait()
        return carry

    lax.fori_loop(1, n_tensor, wait_give, 0)

    def wait_gather(step, carry):
        gather(step).wait_send()
        return carry

    lax.fori_loop(1, n_resp, wait_gather, 0)
    att_out.wait()
    dq_out.wait()


def per_device(
    n_resp, n_tensor, queries, resp_keys, resp_values, prompt_keys, prompt_values, out_grad, lengths
):
    _, seq, width = queries.shape
    heads = width // HD
    share, wide = prompt_keys.shape
    blocks = seq // CHUNK
    steps = n_resp + blocks
    hbm = pl.BlockSpec(memory_space=pl.ANY)
    vmem = pl.BlockSpec(memory_space=pltpu.VMEM)
    dma = pltpu.SemaphoreType.DMA
    shape = jax.ShapeDtypeStruct
    z_size = 4 if n_resp % 4 == 0 else n_resp
    results = pl.pallas_call(
        functools.partial(kernel, (n_resp, n_tensor, z_size, heads)),
        out_shape=(
            shape((seq, width), BF16),
            shape((seq, width), BF16),
            shape((seq, HD), BF16),
            shape((seq, HD), BF16),
            shape((share, wide), F32),
            shape((share, wide), F32),
        ),
        in_specs=[pl.BlockSpec(memory_space=pltpu.SMEM)] + [hbm] * 6,
        out_specs=(hbm, hbm, vmem, vmem, vmem, vmem),
        scratch_shapes=[
            pltpu.VMEM((seq, width), BF16),
            pltpu.VMEM((seq, width), BF16),
            pltpu.VMEM((seq, HD), BF16),
            pltpu.VMEM((seq, HD), BF16),
            pltpu.VMEM((heads, 2 * HD, seq), BF16),
            pltpu.VMEM((heads, HD, seq), BF16),
            pltpu.VMEM((steps, HD, CHUNK), BF16),
            pltpu.VMEM((steps, HD + ONES, CHUNK), BF16),
            pltpu.VMEM((steps * CHUNK, 2 * HD), BF16),
            pltpu.VMEM((n_resp, 2, CHUNK, HD), BF16),
            pltpu.VMEM((steps, heads, CHUNK, seq), BF16),
            pltpu.VMEM((steps, heads, 8, seq), F32),
            pltpu.VMEM((heads, 8, seq), F32),
            pltpu.VMEM((heads, 8, seq), F32),
            pltpu.VMEM((heads, 8, seq), F32),
            pltpu.VMEM((heads, HD + ONES, seq), F32),
            pltpu.VMEM((heads, HD, seq), F32),
            pltpu.VMEM((seq, width), BF16),
            pltpu.VMEM((seq, width), BF16),
            pltpu.VMEM((2, max(PAIR * CHUNK, seq), seq), F32),
            pltpu.VMEM((2, CHUNK, seq), BF16),
            pltpu.VMEM((2, CHUNK, seq), BF16),
            pltpu.VMEM((2, 8, seq), F32),
            pltpu.VMEM((2, 8, seq), F32),
            pltpu.VMEM((2, CHUNK, HD), F32),
            pltpu.VMEM((n_resp, 2, CHUNK, HD), BF16),
            pltpu.VMEM((n_resp, 2, CHUNK, HD), BF16),
            pltpu.VMEM((2, CHUNK, HD), F32),
            dma((6,)),
            dma((2,)),
            dma((n_tensor, 2)),
            dma((n_tensor, 2)),
            dma((n_resp,)),
            dma((n_resp,)),
            dma((n_resp,)),
            dma((n_resp,)),
            dma((n_tensor, 2)),
            dma((n_tensor, 2)),
        ],
        compiler_params=pltpu.CompilerParams(
            collective_id=0, has_side_effects=True, vmem_limit_bytes=60 * 2**20
        ),
    )(
        lengths,
        queries[0],
        out_grad[0],
        resp_keys[0],
        resp_values[0],
        prompt_keys,
        prompt_values,
    )
    attended, query_grad, key_grad, value_grad, prompt_key_grad, prompt_value_grad = results
    return (
        attended[None],
        query_grad[None],
        key_grad[None],
        value_grad[None],
        prompt_key_grad,
        prompt_value_grad,
    )


def solution(mesh):
    rows = P(("group", "resp"), None, "tensor")
    cached = P(("group", "resp", "tensor"), None)
    return jax.shard_map(
        functools.partial(per_device, mesh.shape["resp"], mesh.shape["tensor"]),
        mesh=mesh,
        in_specs=(rows, rows, rows, cached, cached, rows, P(("group", "resp"))),
        out_specs=(rows, rows, rows, rows, cached, cached),
        check_vma=False,
    )
```

```python
import functools
import math

import jax
import jax.numpy as jnp
from jax import lax
from jax.experimental import pallas as pl
from jax.experimental.pallas import tpu as pltpu
from jax.sharding import PartitionSpec as P

HD = 128
CHUNK = 256
PAIR = 2
ONES = 16
VMEM_BYTES = 54 * 2**20
SCALE = HD**-0.5
LOG_SCALE = SCALE / math.log(2.0)
BF16 = jnp.bfloat16
F32 = jnp.float32
MESH = pl.DeviceIdType.MESH


def mm(left, right):
    return jnp.dot(left, right, preferred_element_type=F32)


def by_tile(op, wide, stat):
    rows, lanes = wide.shape
    return op(wide.reshape(rows // 8, 8, lanes), stat[None]).reshape(rows, lanes)


def top_of(wide):
    rows, lanes = wide.shape
    return jnp.max(wide.reshape(rows // 8, 8, lanes), axis=0)


def hop(step, z_size):
    inner = step % z_size
    return step // z_size, ((inner + 1) // 2) * (2 * (inner % 2) - 1)


def kernel(
    sizes,
    length_ref,
    q_hbm,
    g_hbm,
    rk_hbm,
    rv_hbm,
    pk_hbm,
    pv_hbm,
    att,
    dq,
    drk_ref,
    drv_ref,
    dp_ref,
    q,
    g,
    rk,
    rv,
    q_t,
    g_t,
    k_t,
    v_t,
    k_two,
    cache,
    weights,
    tops,
    top,
    inv_total,
    delta,
    out_t,
    dq_t,
    score_buf,
    w_buf,
    ds_buf,
    stat_a,
    stat_b,
    acc,
    send_buf,
    recv_buf,
    total,
    own_kv,
    rounded,
    returned,
    in_sem,
    a_send,
    a_recv,
    b_send,
    b_recv,
    c_send,
    c_recv,
    d_send,
    d_recv,
):
    n_resp, n_tensor, z_size, heads = sizes
    y_size = n_resp // z_size
    seq = q.shape[0]
    share = pk_hbm.shape[0]
    resp = lax.axis_index("resp")
    tensor = lax.axis_index("tensor")
    y, z = resp // z_size, resp % z_size

    def sends_to(step):
        dy, dz = hop(step, z_size)
        return ((y + dy) % y_size) * z_size + (z + dz + z_size) % z_size

    def comes_from(step):
        dy, dz = hop(step, z_size)
        return ((y - dy + y_size) % y_size) * z_size + (z - dz + z_size) % z_size

    def chunk_at(dy, dz):
        return ((y + dy) % y_size) * z_size + (z + dz + z_size) % z_size

    def columns(index):
        return pl.ds(pl.multiple_of(index * HD, HD), HD)

    def part(index):
        return pl.ds(pl.multiple_of(index * share, share), share)

    loads = [
        pltpu.make_async_copy(source, target, in_sem.at[index])
        for index, (source, target) in enumerate(
            (
                (pk_hbm, own_kv.at[0]),
                (pv_hbm, own_kv.at[1]),
                (q_hbm, q),
                (g_hbm, g),
                (rk_hbm, rk),
                (rv_hbm, rv),
            )
        )
    ]
    for load in loads:
        load.start()

    barrier = pltpu.get_barrier_semaphore()

    def greet(target):
        pl.semaphore_signal(barrier, inc=1, device_id=target, device_id_type=MESH)

    def greet_tensor(step, carry):
        peer = (tensor + step) % n_tensor
        greet({"tensor": peer})
        greet({"tensor": peer, "resp": chunk_at(0, 1)})
        greet({"tensor": peer, "resp": chunk_at(0, -1)})
        return carry

    def greet_resp(step, carry):
        greet({"resp": sends_to(step)})
        return carry

    lax.fori_loop(1, n_tensor, greet_tensor, 0)
    lax.fori_loop(1, n_resp, greet_resp, 0)
    loads[0].wait()
    loads[1].wait()
    pl.semaphore_wait(barrier, 3 * (n_tensor - 1) + n_resp - 1)

    def spread(side, step):
        peer = (tensor + step) % n_tensor
        target = {"tensor": peer}
        if side:
            target["resp"] = chunk_at(0, (0, 1, -1)[side])
        return pltpu.make_async_remote_copy(
            src_ref=own_kv.at[:, :, columns(peer)],
            dst_ref=cache.at[resp, :, part(tensor)],
            send_sem=a_send.at[side, step],
            recv_sem=a_recv.at[side, step],
            device_id=target,
            device_id_type=MESH,
        )

    def arrival(side, step):
        peer = (tensor - step + n_tensor) % n_tensor
        chunk = cache.at[chunk_at(0, (0, -1, 1)[side]), :, part(peer)]
        return pltpu.make_async_remote_copy(
            src_ref=chunk,
            dst_ref=chunk,
            send_sem=a_send.at[side, step],
            recv_sem=a_recv.at[side, step],
            device_id={"tensor": peer},
            device_id_type=MESH,
        )

    def relay(slot, chunk, dy, dz):
        return pltpu.make_async_remote_copy(
            src_ref=cache.at[chunk],
            dst_ref=cache.at[chunk],
            send_sem=b_send.at[slot],
            recv_sem=b_recv.at[slot],
            device_id={"resp": chunk_at(dy, dz)},
            device_id_type=MESH,
        )

    routes = {
        3: (chunk_at(0, 0), chunk_at(0, 2), 0, 2),
        4: (chunk_at(0, 0), chunk_at(1, 0), 1, 0),
        5: (chunk_at(1, 0), chunk_at(1, -1), 0, 1),
        6: (chunk_at(1, 0), chunk_at(1, 1), 0, -1),
        7: (chunk_at(0, 2), chunk_at(1, 2), 1, 0),
    }
    relays = {slot: relay(slot, out, dy, dz) for slot, (out, _, dy, dz) in routes.items()}
    arrivals = {slot: relay(slot, got, dy, dz) for slot, (_, got, dy, dz) in routes.items()}

    def pass_on(waited, begun):
        for slot in waited:
            arrivals[slot].wait_recv()
        for slot in begun:
            relays[slot].start()

    def start_spread(step, carry):
        spread(0, step).start()
        return carry

    def start_sides(step, carry):
        spread(1, step).start()
        spread(2, step).start()
        return carry

    lax.fori_loop(1, n_tensor, start_spread, 0)

    length = length_ref[0]
    live_rows = lax.broadcasted_iota(jnp.int32, (seq, 1), 0) < length
    live_lanes = lax.broadcasted_iota(jnp.int32, (1, seq), 1) < length

    cache[resp, 0, part(tensor), :] = own_kv[0, :, columns(tensor)]
    cache[resp, 1, part(tensor), :] = own_kv[1, :, columns(tensor)]
    for load in loads[2:]:
        load.wait()

    def prepare_head(head, carry):
        wide = q[:, columns(head)].astype(F32).T * LOG_SCALE
        high = wide.astype(BF16)
        q_t[head, 0:HD] = high
        q_t[head, HD:] = (wide - high.astype(F32)).astype(BF16)
        live = jnp.where(live_rows, g[:, columns(head)], jnp.zeros((), BF16))
        g[:, columns(head)] = live
        g_t[head] = live.T
        return carry

    lax.fori_loop(0, heads, prepare_head, 0)
    lax.fori_loop(0, n_tensor, start_sides, 0)

    def wait_spread(step, carry):
        spread(0, step).wait_send()
        arrival(0, step).wait_recv()
        return carry

    def wait_sides(step, carry):
        for side in (1, 2):
            spread(side, step).wait_send()
            arrival(side, step).wait_recv()
        return carry

    def prepare_keys(step, keys, values):
        k_t[step] = keys.T
        v_t[step, 0:HD] = values.T
        v_t[step, HD:] = jnp.ones((ONES, CHUNK), BF16)
        rows = pl.ds(pl.multiple_of(step * CHUNK, CHUNK), CHUNK)
        k_two[rows, 0:HD] = keys
        k_two[rows, HD:] = keys

    key_at = lax.broadcasted_iota(jnp.int32, (CHUNK, CHUNK), 0)
    row_at = lax.broadcasted_iota(jnp.int32, (CHUNK, CHUNK), 1)
    seen = key_at <= row_at

    blocks = seq // CHUNK
    for block in range(blocks):
        rows = slice(block * CHUNK, (block + 1) * CHUNK)
        prepare_keys(n_resp + block, rk[rows, :], rv[rows, :])

    lax.fori_loop(1, n_tensor, wait_spread, 0)
    pass_on((), (3, 4))
    prepare_keys(0, cache[resp, 0], cache[resp, 1])

    near = [(0, 0, False)] + [(n_resp + block, block * CHUNK, True) for block in range(blocks)]

    def staged(stages):
        depth = len(stages)
        for turn in range(heads + depth - 1):
            for late, stage in enumerate(stages):
                if 0 <= turn - late < heads:
                    stage(turn - late)

    def own_scores(head):
        slot = head % 2
        highest = [None] * blocks
        for index, (step, low, diagonal) in enumerate(near):
            rows = slice(index * CHUNK, (index + 1) * CHUNK)
            keys = k_two[step * CHUNK : (step + 1) * CHUNK, :]
            for lane in range(low // CHUNK, blocks):
                lanes = slice(lane * CHUNK, (lane + 1) * CHUNK)
                score = mm(keys, q_t[head, :, lanes])
                if diagonal and lane * CHUNK == low:
                    score = jnp.where(seen, score, -jnp.inf)
                score_buf[slot, rows, lanes] = score
                block_top = top_of(score)
                old = highest[lane]
                highest[lane] = block_top if old is None else jnp.maximum(old, block_top)
        highest = jnp.concatenate(highest, axis=1)
        highest = jnp.broadcast_to(jnp.max(highest, axis=0, keepdims=True), highest.shape)
        top[head] = highest
        for step, _, _ in near:
            tops[step, head] = highest

    def own_weights(head):
        slot = head % 2
        for index, (step, low, _) in enumerate(near):
            rows = slice(index * CHUNK, (index + 1) * CHUNK)
            shift = tops[step, head, :, low:seq]
            power = jnp.exp2(by_tile(jnp.subtract, score_buf[slot, rows, low:seq], shift))
            weights[step, head, :, low:seq] = power.astype(BF16)

    def own_mix(head):
        for index, (step, low, _) in enumerate(near):
            term = mm(v_t[step], weights[step, head, :, low:seq])
            if index == 0:
                out_t[head] = term
            else:
                out_t[head, :, low:seq] += term

    staged((own_scores, own_weights, own_mix))

    def forward(first, count):
        for index in range(count):
            step = first + index
            source = comes_from(step)
            prepare_keys(step, cache[source, 0], cache[source, 1])

        def scores(head):
            slot = head % 2
            highest = None
            for index in range(count):
                at = pl.ds(pl.multiple_of((first + index) * CHUNK, CHUNK), CHUNK)
                score = mm(k_two[at, :], q_t[head])
                score_buf[slot, index * CHUNK : (index + 1) * CHUNK] = score
                block_top = top_of(score)
                highest = block_top if highest is None else jnp.maximum(highest, block_top)
            old = top[head]
            new = jnp.maximum(old, jnp.max(highest, axis=0, keepdims=True))
            top[head] = new
            stat_a[slot] = jnp.exp2(old - new)
            for index in range(count):
                tops[first + index, head] = new

        def powers(head):
            slot = head % 2
            shift = tops[first, head]
            for index in range(count):
                score = score_buf[slot, index * CHUNK : (index + 1) * CHUNK]
                power = jnp.exp2(by_tile(jnp.subtract, score, shift))
                weights[first + index, head] = power.astype(BF16)
            stat_b[slot] = stat_a[slot]

        def mix(head):
            term = mm(v_t[first], weights[first, head])
            for index in range(1, count):
                term = term + mm(v_t[first + index], weights[first + index, head])
            out_t[head] = by_tile(jnp.multiply, out_t[head], stat_b[head % 2]) + term

        staged((scores, powers, mix))

    lax.fori_loop(0, n_tensor, wait_sides, 0)

    def forward_single(step, carry):
        pl.when(step == 2)(functools.partial(pass_on, (4,), (5, 6)))
        forward(step, 1)
        return carry

    lax.fori_loop(1, 3, forward_single, 0)

    def forward_turn(turn, carry):
        pl.when(turn == 0)(functools.partial(pass_on, (3,), (7,)))
        pl.when(turn == 1)(functools.partial(pass_on, (5, 6), ()))
        forward(3 + turn * PAIR, PAIR)
        return carry

    lax.fori_loop(0, 2, forward_turn, 0)
    pass_on((7,), ())
    forward(n_resp - 1, 1)

    def close_head(head, carry):
        inverse = 1.0 / out_t[head, HD : HD + 1]
        inv_total[head] = jnp.broadcast_to(inverse, (8, seq))
        done = jnp.where(live_lanes, out_t[head, 0:HD] * inverse, 0.0).astype(BF16)
        row_delta = jnp.sum(
            done.astype(F32) * g_t[head].astype(F32), axis=0, keepdims=True
        )
        delta[head] = jnp.broadcast_to(row_delta, (8, seq))
        att[:, columns(head)] = done.T
        dq_t[head] = jnp.zeros((HD, seq), F32)
        return carry

    lax.fori_loop(0, heads, close_head, 0)
    def backward_chunk(step, values, low, *more):
        lanes = slice(low, seq)
        width = seq - low

        def products(head):
            slot = head % 2
            score_buf[slot, 0:CHUNK, 0:width] = mm(values, g_t[head, :, lanes])
            stat_a[slot, :, 0:width] = (
                jnp.exp2(tops[step, head, :, lanes] - top[head, :, lanes])
                * inv_total[head, :, lanes]
            )

        def grads(head):
            slot = head % 2
            weight = by_tile(
                jnp.multiply,
                weights[step, head, :, lanes].astype(F32),
                stat_a[slot, :, 0:width],
            )
            w_buf[slot, :, 0:width] = weight.astype(BF16)
            gap = by_tile(
                jnp.subtract, score_buf[slot, 0:CHUNK, 0:width], delta[head, :, lanes]
            )
            ds_buf[slot, :, 0:width] = (weight * gap).astype(BF16)

        def terms(head):
            slot = head % 2
            score_grad = ds_buf[slot, :, 0:width]
            dq_t[head, :, lanes] += mm(k_t[step], score_grad)
            at = slice(head * HD, (head + 1) * HD)
            key_term = mm(score_grad, q[lanes, at])
            value_term = mm(w_buf[slot, :, 0:width], g[lanes, at])
            if head == 0:
                acc[0] = key_term
                acc[1] = value_term
            else:
                acc[0] += key_term
                acc[1] += value_term

        staged((products, grads, terms) + more)

    def collect(step):
        return pltpu.make_async_remote_copy(
            src_ref=send_buf.at[step],
            dst_ref=recv_buf.at[step],
            send_sem=c_send.at[step],
            recv_sem=c_recv.at[step],
            device_id={"resp": comes_from(step)},
            device_id_type=MESH,
        )

    def backward(turn, carry):
        step = n_resp - 1 - turn
        backward_chunk(step, cache[comes_from(step), 1], 0)

        @pl.when(step > 0)
        def _():
            send_buf[step, 0] = (acc[0] * SCALE).astype(BF16)
            send_buf[step, 1] = acc[1].astype(BF16)
            collect(step).start()

        @pl.when(step == 0)
        def _():
            total[0] = acc[0] * SCALE
            total[1] = acc[1]

        return carry

    lax.fori_loop(0, n_resp, backward, 0)

    def backward_own(block, *more):
        rows = slice(block * CHUNK, (block + 1) * CHUNK)
        backward_chunk(n_resp + block, rv[rows, :], block * CHUNK, *more)
        drk_ref[rows, :] = (acc[0] * SCALE).astype(BF16)
        drv_ref[rows, :] = acc[1].astype(BF16)

    for block in range(1, blocks):
        backward_own(block)

    def add_part(step, carry):
        collect(step).wait()
        total[0] += recv_buf[step, 0].astype(F32)
        total[1] += recv_buf[step, 1].astype(F32)
        return carry

    lax.fori_loop(1, n_resp, add_part, 0)
    rounded[...] = total[...].astype(BF16)

    def give_back(step):
        peer = (tensor + step) % n_tensor
        return pltpu.make_async_remote_copy(
            src_ref=rounded.at[:, part(peer)],
            dst_ref=returned.at[:, :, columns(tensor)],
            send_sem=d_send.at[step],
            recv_sem=d_recv.at[step],
            device_id={"tensor": peer},
            device_id_type=MESH,
        )

    def start_give(step, carry):
        give_back(step).start()
        return carry

    lax.fori_loop(1, n_tensor, start_give, 0)
    returned[0, :, columns(tensor)] = rounded[0, part(tensor), :]
    returned[1, :, columns(tensor)] = rounded[1, part(tensor), :]

    def close_query(head):
        dq[:, head * HD : (head + 1) * HD] = (dq_t[head] * SCALE).astype(BF16).T

    backward_own(0, close_query)

    def wait_give(step, carry):
        give_back(step).wait()
        return carry

    lax.fori_loop(1, n_tensor, wait_give, 0)
    dp_ref[...] = returned[...].astype(F32)

    for copy in relays.values():
        copy.wait_send()


def deliver(att, dq, drk, drv, dp, *rest):
    outputs, sems = rest[:-1], rest[-1]
    copies = [
        pltpu.make_async_copy(source, target, sems.at[index])
        for index, (source, target) in enumerate(
            zip((att, dq, drk, drv, dp.at[0], dp.at[1]), outputs)
        )
    ]
    for copy in copies:
        copy.start()
    for copy in copies:
        copy.wait()


def per_device(
    n_resp, n_tensor, queries, resp_keys, resp_values, prompt_keys, prompt_values, out_grad, lengths
):
    _, seq, width = queries.shape
    heads = width // HD
    share, wide = prompt_keys.shape
    blocks = seq // CHUNK
    steps = n_resp + blocks
    hbm = pl.BlockSpec(memory_space=pl.ANY)
    vmem = pl.BlockSpec(memory_space=pltpu.VMEM)
    dma = pltpu.SemaphoreType.DMA
    shape = jax.ShapeDtypeStruct
    z_size = 4 if n_resp % 4 == 0 else n_resp
    outputs = (
        ((seq, width), BF16),
        ((seq, width), BF16),
        ((seq, HD), BF16),
        ((seq, HD), BF16),
        ((share, wide), F32),
        ((share, wide), F32),
    )
    kept = outputs[:4] + (((2, share, wide), F32),)
    results = pl.pallas_call(
        functools.partial(kernel, (n_resp, n_tensor, z_size, heads)),
        out_shape=tuple(pltpu.VMEM(size, kind) for size, kind in kept),
        in_specs=[pl.BlockSpec(memory_space=pltpu.SMEM)] + [hbm] * 6,
        out_specs=(vmem,) * len(kept),
        scratch_shapes=[
            pltpu.VMEM((seq, width), BF16),
            pltpu.VMEM((seq, width), BF16),
            pltpu.VMEM((seq, HD), BF16),
            pltpu.VMEM((seq, HD), BF16),
            pltpu.VMEM((heads, 2 * HD, seq), BF16),
            pltpu.VMEM((heads, HD, seq), BF16),
            pltpu.VMEM((steps, HD, CHUNK), BF16),
            pltpu.VMEM((steps, HD + ONES, CHUNK), BF16),
            pltpu.VMEM((steps * CHUNK, 2 * HD), BF16),
            pltpu.VMEM((n_resp, 2, CHUNK, HD), BF16),
            pltpu.VMEM((steps, heads, CHUNK, seq), BF16),
            pltpu.VMEM((steps, heads, 8, seq), F32),
            pltpu.VMEM((heads, 8, seq), F32),
            pltpu.VMEM((heads, 8, seq), F32),
            pltpu.VMEM((heads, 8, seq), F32),
            pltpu.VMEM((heads, HD + ONES, seq), F32),
            pltpu.VMEM((heads, HD, seq), F32),
            pltpu.VMEM((2, max(PAIR * CHUNK, CHUNK + seq), seq), F32),
            pltpu.VMEM((2, CHUNK, seq), BF16),
            pltpu.VMEM((2, CHUNK, seq), BF16),
            pltpu.VMEM((2, 8, seq), F32),
            pltpu.VMEM((2, 8, seq), F32),
            pltpu.VMEM((2, CHUNK, HD), F32),
            pltpu.VMEM((n_resp, 2, CHUNK, HD), BF16),
            pltpu.VMEM((n_resp, 2, CHUNK, HD), BF16),
            pltpu.VMEM((2, CHUNK, HD), F32),
            pltpu.VMEM((2, share, wide), BF16),
            pltpu.VMEM((2, CHUNK, HD), BF16),
            pltpu.VMEM((2, share, wide), BF16),
            dma((6,)),
            dma((3, n_tensor)),
            dma((3, n_tensor)),
            dma((n_resp,)),
            dma((n_resp,)),
            dma((n_resp,)),
            dma((n_resp,)),
            dma((n_tensor,)),
            dma((n_tensor,)),
        ],
        compiler_params=pltpu.CompilerParams(
            collective_id=0, has_side_effects=True, vmem_limit_bytes=VMEM_BYTES
        ),
    )(
        lengths,
        queries[0],
        out_grad[0],
        resp_keys[0],
        resp_values[0],
        prompt_keys,
        prompt_values,
    )
    results = pl.pallas_call(
        deliver,
        out_shape=tuple(shape(size, kind) for size, kind in outputs),
        in_specs=[vmem] * len(kept),
        out_specs=(hbm,) * len(outputs),
        scratch_shapes=[dma((len(outputs),))],
        compiler_params=pltpu.CompilerParams(vmem_limit_bytes=2**20),
    )(*results)
    attended, query_grad, key_grad, value_grad, prompt_key_grad, prompt_value_grad = results
    return (
        attended[None],
        query_grad[None],
        key_grad[None],
        value_grad[None],
        prompt_key_grad,
        prompt_value_grad,
    )


def solution(mesh):
    rows = P(("group", "resp"), None, "tensor")
    cached = P(("group", "resp", "tensor"), None)
    return jax.shard_map(
        functools.partial(per_device, mesh.shape["resp"], mesh.shape["tensor"]),
        mesh=mesh,
        in_specs=(rows, rows, rows, cached, cached, rows, P(("group", "resp"))),
        out_specs=(rows, rows, rows, rows, cached, cached),
        check_vma=False,
    )
```
